32 devices in a mesh: groups: 2 (over y), ctx: 16 (over z, x, core).
Axes of the slice: x: 2, y: 2, z: 4, core: 2. Of those that a mesh axis runs over, the one named last changes fastest.
Arguments:
- queries: bfloat16 [512, 6144], P(('groups', 'ctx')), parts along dimension 0, may hold values from -8 to 8
- latents: bfloat16 [4096, 576], P(('groups', 'ctx')), parts along dimension 0, may hold values from -8 to 8
- w_uk: bfloat16 [32, 128, 512], replicated, may hold values from -0.5 to 0.5
- w_uv: bfloat16 [32, 512, 128], replicated, may hold values from -1.5 to 1.5
Outputs:
- attended: bfloat16 [512, 4096], P(('groups', 'ctx')), parts along dimension 0
The draws below stay inside these ranges and needn't reach their ends.
There are 2 independent parts, one for each index of `groups`. The reference program is written for one: setup_inputs(seed, part) draws one part's arguments, and reference() takes and returns one part's arrays. A program takes and returns all parts, laid end to end along the dimension named above; an argument that names none is the same for every part. Nothing has to cross between parts.
All inputs are finite; a program needn't handle non-finite values.
Results may differ from the reference program's by a relative error of at most 0.008.
Values may be sent and summed in bfloat16 or wider, within the bound.
A program may use at most 128 MiB of HBM per device.

```python
import jax
import jax.numpy as jnp
from jax import lax

HEADS = 32
NOPE = 128
ROPE = 64
RANK = 512
VDIM = 128
TOK_DEV = 128
QRY_DEV = 16
TOKENS = 2048
QUERIES = 256


def draw_queries(key, part):
    base_key = jax.random.fold_in(key, 11)
    shape = (QUERIES, HEADS, NOPE + ROPE)
    values = jnp.clip(jax.random.normal(base_key, shape, jnp.float32), -4.0, 4.0)
    return values.reshape(QUERIES, HEADS * (NOPE + ROPE)).astype(jnp.bfloat16)


def draw_latents(key, part):
    base_key = jax.random.fold_in(key, 21)
    shape = (TOKENS, RANK + ROPE)
    values = jnp.clip(jax.random.normal(base_key, shape, jnp.float32), -4.0, 4.0)
    return values.astype(jnp.bfloat16)


def normal_values(own_key, dims, width, limit, held_as=jnp.bfloat16):
    return jnp.clip(width * jax.random.normal(own_key, dims, jnp.float32), -limit, limit).astype(held_as)


def setup_inputs(seed: int = 0, part: int = 0) -> dict:
    keys = jax.random.split(jax.random.key(seed), 5)
    own_keys = jax.random.split(jax.random.fold_in(keys[4], part), 5)
    queries = draw_queries(jax.random.fold_in(jax.random.fold_in(keys[4], part), 71), part)
    latents = draw_latents(jax.random.fold_in(jax.random.fold_in(keys[4], part), 71), part)
    w_uk = normal_values(keys[2], (HEADS, NOPE, RANK), NOPE ** -0.5, 0.5)
    w_uv = normal_values(keys[3], (HEADS, RANK, VDIM), 0.25, 1.5)
    return dict(queries=queries, latents=latents, w_uk=w_uk, w_uv=w_uv)


def reference(queries, latents, w_uk, w_uv):
    shaped = queries.reshape(QUERIES, HEADS, NOPE + ROPE)
    q_nope = shaped[:, :, :NOPE]
    q_rope = shaped[:, :, NOPE:]
    q_lat = jnp.einsum('thi,hil->thl', q_nope.astype(jnp.float32), w_uk.astype(jnp.float32)).astype(jnp.bfloat16)
    key_nope = latents[:, :RANK].astype(jnp.float32)
    key_rope = latents[:, RANK:].astype(jnp.float32)
    scale = 1.0 / jnp.sqrt(jnp.float32(NOPE + ROPE))
    key_pos = jnp.arange(TOKENS, dtype=jnp.int32)
    block_rows = min(64, QUERIES)

    def one_block(start):
        lat_block = lax.dynamic_slice_in_dim(q_lat, start, block_rows, 0).astype(jnp.float32)
        rope_block = lax.dynamic_slice_in_dim(q_rope, start, block_rows, 0).astype(jnp.float32)
        score = jnp.einsum('thl,jl->thj', lat_block, key_nope) + jnp.einsum('thr,jr->thj', rope_block, key_rope)
        score = score * scale
        row_ids = start + jnp.arange(block_rows, dtype=jnp.int32)
        query_pos = row_ids // QRY_DEV * TOK_DEV + TOK_DEV - QRY_DEV + row_ids % QRY_DEV
        allowed = key_pos[None, None, :] <= query_pos[:, None, None]
        score = jnp.where(allowed, score, -jnp.inf)
        top = lax.optimization_barrier(jnp.max(score, axis=-1, keepdims=True))
        expo = jnp.exp(score - top)
        total = lax.optimization_barrier(jnp.sum(expo, axis=-1))
        weight = expo.astype(jnp.bfloat16).astype(jnp.float32)
        o_lat = (jnp.einsum('thj,jl->thl', weight, key_nope) / total[:, :, None]).astype(jnp.bfloat16)
        result = jnp.einsum('thl,hlc->thc', o_lat.astype(jnp.float32), w_uv.astype(jnp.float32))
        return result.astype(jnp.bfloat16)
    starts = jnp.arange(0, QUERIES, block_rows, dtype=jnp.int32)
    blocks = lax.map(one_block, starts)
    return blocks.reshape(QUERIES, HEADS * VDIM)
```

```python
import functools
import math

import jax
import jax.numpy as jnp
from jax import lax
from jax.experimental import pallas as pl
from jax.experimental.pallas import tpu as pltpu
from jax.sharding import PartitionSpec as P

CORES = 2
MESH = pl.DeviceIdType.MESH


def grid_of(count):
    chips = count // CORES
    wide = 1 << (int(math.log2(chips)) // 3)
    return chips // wide, wide


def kernel(
    deep, wide, heads, nope, rank,
    queries, latents, w_uk, w_uv, out,
    keys, raw, q_all, uk, uv, top, total, acc,
    up_sem, side_sem, twin_sem, pass_sem, recv_sem, local_sem, uk_sem,
):
    index = lax.axis_index("ctx")
    core = lax.rem(index, CORES)
    x = lax.rem(index // CORES, wide)
    z = index // (CORES * wide)
    rows = out.shape[0]
    krows = latents.shape[0]
    width = raw.shape[1] // heads
    vdim = out.shape[1] // heads
    span = CORES * krows
    factor = math.log2(math.e) / math.sqrt(width)

    def place(zz, xx, cc):
        return (zz * wide + xx) * CORES + cc

    def slot(block):
        return keys.at[pl.ds(pl.multiple_of(block * krows, krows), krows), :]

    def copy(block, target, send_sem, own=False):
        return pltpu.make_async_remote_copy(
            src_ref=latents if own else slot(block),
            dst_ref=slot(block),
            send_sem=send_sem,
            recv_sem=recv_sem.at[block],
            device_id={"ctx": target},
            device_id_type=MESH,
        )

    twin = place(z, x, 1 - core)
    above = place(lax.rem(z + 1, deep), x, core)
    below = place(lax.rem(z + deep - 1, deep), x, core)
    sides = [lax.rem(x + d, wide) for d in range(1, wide)]

    groups = uk_sem.shape[0]
    per = heads // groups
    raw_copy = pltpu.make_async_copy(queries, raw, local_sem.at[0])
    raw_copy.start()
    uk_copies = []
    for g in range(groups):
        part = pl.ds(g * per, per)
        uk_copies.append(pltpu.make_async_copy(w_uk.at[part], uk.at[part], uk_sem.at[g]))
        uk_copies[-1].start()
    own_copy = pltpu.make_async_copy(latents, slot(index), local_sem.at[1])
    own_copy.start()

    barrier = pltpu.get_barrier_semaphore()

    def greet(target):
        pl.semaphore_signal(barrier, inc=1, device_id={"ctx": target}, device_id_type=MESH)

    greet(twin)
    for side in sides:
        greet(place(z, side, core))

    @pl.when(z + 1 < deep)
    def _():
        greet(above)

    @pl.when(z > 0)
    def _():
        greet(below)

    ends = (z + 1 < deep).astype(jnp.int32) + (z > 0).astype(jnp.int32)
    pl.semaphore_wait(barrier, wide + ends)

    def spread(step, block, own, act):
        @pl.when(z + 1 < deep)
        def _():
            act(copy(block, above, up_sem.at[step], own))

        for d, side in enumerate(sides):
            def to_side():
                act(copy(block, place(z, side, core), side_sem.at[step, d], own))

            if own:
                pl.when(side > x)(to_side)
            else:
                to_side()
        act(copy(block, twin, twin_sem.at[step], own))

    def arrived(block):
        copy(block, twin, twin_sem.at[0]).wait_recv()

    spread(0, index, True, lambda c: c.start())

    raw_copy.wait()
    uv_copy = pltpu.make_async_copy(w_uv, uv, local_sem.at[2])
    for h in range(heads):
        if h % per == 0:
            uk_copies[h // per].wait()
        query = raw[:, h * width:(h + 1) * width]
        lat = jnp.dot(query[:, :nope], uk[h], preferred_element_type=jnp.float32)
        q_all[h * rows:(h + 1) * rows, :rank] = lat.astype(jnp.bfloat16)
        q_all[h * rows:(h + 1) * rows, rank:] = query[:, nope:]
    uv_copy.start()

    parts = 4
    high = heads * rows // parts

    def attend(pair, first):
        start = pl.multiple_of(pair * span, span)
        key = keys[pl.ds(start, span), :]
        value = key[:, :rank]
        for part in range(parts):
            own = pl.ds(part * high, high)
            score = lax.dot_general(
                q_all[own, :], key, (((1,), (1,)), ((), ())), preferred_element_type=jnp.float32
            )
            if first:
                row = lax.broadcasted_iota(jnp.int32, score.shape, 0)
                col = lax.broadcasted_iota(jnp.int32, score.shape, 1)
                limit = core * krows + krows - rows + lax.rem(row, rows)
                score = jnp.where(col <= limit, score, -jnp.inf)
            best = jnp.max(score, axis=1, keepdims=True)
            if not first:
                old = top[own, :1]
                best = jnp.maximum(old, best)
            expo = jnp.exp2((score - best) * factor)
            lanes = expo[:, :128]
            for lane in range(128, span, 128):
                lanes = lanes + expo[:, lane:lane + 128]
            gain = jnp.dot(expo.astype(jnp.bfloat16), value, preferred_element_type=jnp.float32)
            if first:
                total[own, :] = lanes
                acc[own, :] = gain
            else:
                shrink = jnp.exp2((old - best) * factor)
                total[own, :] = total[own, :] * shrink + lanes
                acc[own, :] = acc[own, :] * shrink + gain
            top[own, :] = jnp.broadcast_to(best, (high, 128))

    own_copy.wait()
    arrived(twin)
    attend(index // CORES, True)

    def step_of(step, carry):
        @pl.when(step <= z)
        def _():
            block = place(z - step, x, core)
            arrived(block)
            spread(step, block, False, lambda c: c.start())
            arrived(place(z - step, x, 1 - core))
            attend((z - step) * wide + x, False)

        back = step - 1
        for d, side in enumerate(sides):
            @pl.when(jnp.logical_or(back >= 1, side < x))
            def _():
                block = place(z - back, side, core)
                arrived(block)
                copy(block, twin, pass_sem.at[back, d]).start()
                arrived(place(z - back, side, 1 - core))
                attend((z - back) * wide + side, False)
        return carry

    lax.fori_loop(1, z + 2, step_of, 0)

    uv_copy.wait()
    for h in range(heads):
        own = pl.ds(h * rows, rows)
        whole = jnp.sum(total[own, :], axis=1, keepdims=True)
        mixed = (acc[own, :] * (1.0 / whole)).astype(jnp.bfloat16)
        out[:, h * vdim:(h + 1) * vdim] = jnp.dot(
            mixed, uv[h], preferred_element_type=jnp.float32
        ).astype(out.dtype)

    spread(0, index, True, lambda c: c.wait_send())

    def drain(step, carry):
        @pl.when(step <= z)
        def _():
            spread(step, place(z - step, x, core), False, lambda c: c.wait_send())

        back = step - 1
        for d, side in enumerate(sides):
            @pl.when(jnp.logical_or(back >= 1, side < x))
            def _():
                copy(place(z - back, side, core), twin, pass_sem.at[back, d]).wait_send()
        return carry

    lax.fori_loop(1, z + 2, drain, 0)


def body(count, queries, latents, w_uk, w_uv):
    deep, wide = grid_of(count)
    heads, nope, rank = w_uk.shape
    vdim = w_uv.shape[2]
    rows, krows = queries.shape[0], latents.shape[0]
    dma = pltpu.SemaphoreType.DMA
    lanes = max(wide - 1, 1)
    return pl.pallas_call(
        functools.partial(kernel, deep, wide, heads, nope, rank),
        out_shape=jax.ShapeDtypeStruct((rows, heads * vdim), jnp.bfloat16),
        in_specs=[pl.BlockSpec(memory_space=pl.ANY)] * 4,
        out_specs=pl.BlockSpec(memory_space=pltpu.VMEM),
        scratch_shapes=[
            pltpu.VMEM((count * krows, latents.shape[1]), jnp.bfloat16),
            pltpu.VMEM(queries.shape, jnp.bfloat16),
            pltpu.VMEM((heads * rows, latents.shape[1]), jnp.bfloat16),
            pltpu.VMEM(w_uk.shape, jnp.bfloat16),
            pltpu.VMEM(w_uv.shape, jnp.bfloat16),
            pltpu.VMEM((heads * rows, 128), jnp.float32),
            pltpu.VMEM((heads * rows, 128), jnp.float32),
            pltpu.VMEM((heads * rows, rank), jnp.float32),
            dma((deep,)),
            dma((deep, lanes)),
            dma((deep,)),
            dma((deep, lanes)),
            dma((count,)),
            dma((3,)),
            dma((4,)),
        ],
        compiler_params=pltpu.CompilerParams(
            collective_id=0, has_side_effects=True, vmem_limit_bytes=48 * 1024 * 1024
        ),
    )(queries, latents, w_uk, w_uv)


def solution(mesh):
    placed = (P(("groups", "ctx"), None), P(("groups", "ctx"), None), P(), P())
    return jax.shard_map(
        functools.partial(body, mesh.shape["ctx"]),
        mesh=mesh, in_specs=placed, out_specs=P(("groups", "ctx"), None), check_vma=False,
    )
```

```python
import functools
import math

import jax
import jax.numpy as jnp
from jax import lax
from jax.experimental import pallas as pl
from jax.experimental.pallas import tpu as pltpu
from jax.sharding import PartitionSpec as P

CORES = 2
MESH = pl.DeviceIdType.MESH


def grid_of(count):
    chips = count // CORES
    wide = 1 << (int(math.log2(chips)) // 3)
    return chips // wide, wide


def kernel(
    deep, wide, heads, nope, rank,
    queries, latents, w_uk, w_uv, out,
    keys, raw, q_all, uk, uv, top, total, acc,
    up_sem, side_sem, twin_sem, pass_sem, recv_sem, local_sem, uk_sem,
):
    index = lax.axis_index("ctx")
    core = lax.rem(index, CORES)
    x = lax.rem(index // CORES, wide)
    z = index // (CORES * wide)
    rows = out.shape[0]
    krows = latents.shape[1]
    width = raw.shape[1] // heads
    vdim = out.shape[1] // heads
    span = CORES * krows
    factor = math.log2(math.e) / math.sqrt(width)

    def place(zz, xx, cc):
        return (zz * wide + xx) * CORES + cc

    def slot(block):
        return keys.at[block]

    def copy(block, target, send_sem, own=False):
        return pltpu.make_async_remote_copy(
            src_ref=latents if own else slot(block),
            dst_ref=slot(block),
            send_sem=send_sem,
            recv_sem=recv_sem.at[block],
            device_id={"ctx": target},
            device_id_type=MESH,
        )

    twin = place(z, x, 1 - core)
    above = place(lax.rem(z + 1, deep), x, core)
    below = place(lax.rem(z + deep - 1, deep), x, core)
    sides = [lax.rem(x + d, wide) for d in range(1, wide)]

    groups = uk_sem.shape[0]
    per = heads // groups
    raw_copy = pltpu.make_async_copy(queries, raw, local_sem.at[0])
    raw_copy.start()
    uk_copies = []
    for g in range(groups):
        part = pl.ds(g * per, per)
        uk_copies.append(pltpu.make_async_copy(w_uk.at[part], uk.at[part], uk_sem.at[g]))
        uk_copies[-1].start()
    own_copy = pltpu.make_async_copy(latents, slot(index), local_sem.at[1])
    own_copy.start()

    barrier = pltpu.get_barrier_semaphore()

    def greet(target):
        pl.semaphore_signal(barrier, inc=1, device_id={"ctx": target}, device_id_type=MESH)

    greet(twin)
    for side in sides:
        greet(place(z, side, core))

    @pl.when(z + 1 < deep)
    def _():
        greet(above)

    @pl.when(z > 0)
    def _():
        greet(below)

    ends = (z + 1 < deep).astype(jnp.int32) + (z > 0).astype(jnp.int32)
    pl.semaphore_wait(barrier, wide + ends)

    def spread(step, block, own, act):
        @pl.when(z + 1 < deep)
        def _():
            act(copy(block, above, up_sem.at[step], own))

        for d, side in enumerate(sides):
            def to_side():
                act(copy(block, place(z, side, core), side_sem.at[step, d], own))

            if own:
                pl.when(side > x)(to_side)
            else:
                to_side()
        act(copy(block, twin, twin_sem.at[step], own))

    def arrived(block):
        copy(block, twin, twin_sem.at[0]).wait_recv()

    spread(0, index, True, lambda c: c.start())

    raw_copy.wait()
    uv_copy = pltpu.make_async_copy(w_uv, uv, local_sem.at[2])
    for h in range(heads):
        if h % per == 0:
            uk_copies[h // per].wait()
        query = raw[:, h * width:(h + 1) * width]
        lat = jnp.dot(query[:, :nope], uk[h], preferred_element_type=jnp.float32)
        q_all[h * rows:(h + 1) * rows, :rank] = lat.astype(jnp.bfloat16)
        q_all[h * rows:(h + 1) * rows, rank:] = query[:, nope:]
    uv_copy.start()

    parts = 2
    high = heads * rows // parts

    def attend(pair, first):
        blocks = [keys[pair * CORES + c] for c in range(CORES)]
        key = jnp.concatenate(blocks, axis=1)
        value = key[:rank, :].T
        owns = [pl.ds(part * high, high) for part in range(parts)]
        scores = [
            jnp.dot(q_all[own, :], key, preferred_element_type=jnp.float32) for own in owns
        ]
        for own, score in zip(owns, scores):
            if first:
                row = lax.broadcasted_iota(jnp.int32, score.shape, 0)
                col = lax.broadcasted_iota(jnp.int32, score.shape, 1)
                limit = core * krows + krows - rows + lax.rem(row, rows)
                score = jnp.where(col <= limit, score, -jnp.inf)
            best = jnp.max(score, axis=1, keepdims=True)
            if not first:
                old = top[own, :1]
                best = jnp.maximum(old, best)
            expo = jnp.exp2((score - best) * factor)
            lanes = expo[:, :128]
            for lane in range(128, span, 128):
                lanes = lanes + expo[:, lane:lane + 128]
            gain = jnp.dot(expo.astype(jnp.bfloat16), value, preferred_element_type=jnp.float32)
            if first:
                total[own, :] = lanes
                acc[own, :] = gain
            else:
                shrink = jnp.exp2((old - best) * factor)
                total[own, :] = total[own, :] * shrink + lanes
                acc[own, :] = acc[own, :] * shrink + gain
            top[own, :] = jnp.broadcast_to(best, (high, 128))

    own_copy.wait()
    arrived(twin)
    attend(index // CORES, True)

    def step_of(step, carry):
        @pl.when(step <= z)
        def _():
            block = place(z - step, x, core)
            arrived(block)
            spread(step, block, False, lambda c: c.start())
            arrived(place(z - step, x, 1 - core))
            attend((z - step) * wide + x, False)

        back = step - 1
        for d, side in enumerate(sides):
            @pl.when(jnp.logical_or(back >= 1, side < x))
            def _():
                block = place(z - back, side, core)
                arrived(block)
                copy(block, twin, pass_sem.at[back, d]).start()
                arrived(place(z - back, side, 1 - core))
                attend((z - back) * wide + side, False)
        return carry

    lax.fori_loop(1, z + 2, step_of, 0)

    uv_copy.wait()
    for h in range(heads):
        own = pl.ds(h * rows, rows)
        whole = jnp.sum(total[own, :], axis=1, keepdims=True)
        mixed = (acc[own, :] * (1.0 / whole)).astype(jnp.bfloat16)
        out[:, h * vdim:(h + 1) * vdim] = jnp.dot(
            mixed, uv[h], preferred_element_type=jnp.float32
        ).astype(out.dtype)

    spread(0, index, True, lambda c: c.wait_send())

    def drain(step, carry):
        @pl.when(step <= z)
        def _():
            spread(step, place(z - step, x, core), False, lambda c: c.wait_send())

        back = step - 1
        for d, side in enumerate(sides):
            @pl.when(jnp.logical_or(back >= 1, side < x))
            def _():
                copy(place(z - back, side, core), twin, pass_sem.at[back, d]).wait_send()
        return carry

    lax.fori_loop(1, z + 2, drain, 0)


def body(count, queries, latents, w_uk, w_uv):
    deep, wide = grid_of(count)
    heads, nope, rank = w_uk.shape
    vdim = w_uv.shape[2]
    rows = queries.shape[0]
    krows, width = latents.shape
    dma = pltpu.SemaphoreType.DMA
    lanes = max(wide - 1, 1)
    return pl.pallas_call(
        functools.partial(kernel, deep, wide, heads, nope, rank),
        out_shape=jax.ShapeDtypeStruct((rows, heads * vdim), jnp.bfloat16),
        in_specs=[pl.BlockSpec(memory_space=pl.ANY)] * 4,
        out_specs=pl.BlockSpec(memory_space=pltpu.VMEM),
        scratch_shapes=[
            pltpu.VMEM((count, width, krows), jnp.bfloat16),
            pltpu.VMEM(queries.shape, jnp.bfloat16),
            pltpu.VMEM((heads * rows, width), jnp.bfloat16),
            pltpu.VMEM(w_uk.shape, jnp.bfloat16),
            pltpu.VMEM(w_uv.shape, jnp.bfloat16),
            pltpu.VMEM((heads * rows, 128), jnp.float32),
            pltpu.VMEM((heads * rows, 128), jnp.float32),
            pltpu.VMEM((heads * rows, rank), jnp.float32),
            dma((deep,)),
            dma((deep, lanes)),
            dma((deep,)),
            dma((deep, lanes)),
            dma((count,)),
            dma((3,)),
            dma((4,)),
        ],
        compiler_params=pltpu.CompilerParams(
            collective_id=0, has_side_effects=True, vmem_limit_bytes=60 * 1024 * 1024
        ),
    )(queries, latents.T, w_uk, w_uv)


def solution(mesh):
    placed = (P(("groups", "ctx"), None), P(("groups", "ctx"), None), P(), P())
    return jax.shard_map(
        functools.partial(body, mesh.shape["ctx"]),
        mesh=mesh, in_specs=placed, out_specs=P(("groups", "ctx"), None), check_vma=False,
    )
```

```python
import functools
import math

import jax
import jax.numpy as jnp
from jax import lax
from jax.experimental import pallas as pl
from jax.experimental.pallas import tpu as pltpu
from jax.sharding import PartitionSpec as P

CORES = 2
PIECES = 2
MESH = pl.DeviceIdType.MESH


def grid_of(count):
    chips = count // CORES
    wide = 1 << (int(math.log2(chips)) // 3)
    return chips // wide, wide


def kernel(
    deep, wide, heads, nope, rank,
    queries, latents, w_uk, w_uv, out,
    keys, raw, q_all, uk, uv, top, total, acc,
    up_sem, side_sem, twin_sem, pass_sem, recv_sem, local_sem, uk_sem,
):
    index = lax.axis_index("ctx")
    core = lax.rem(index, CORES)
    x = lax.rem(index // CORES, wide)
    z = index // (CORES * wide)
    rows = out.shape[0]
    krows = latents.shape[1]
    width = raw.shape[1] // heads
    vdim = out.shape[1] // heads
    span = CORES * krows
    factor = math.log2(math.e) / math.sqrt(width)

    def place(zz, xx, cc):
        return (zz * wide + xx) * CORES + cc

    def piece_of(piece):
        size = keys.shape[1] // PIECES
        return pl.ds(piece * size, size)

    def copy(block, piece, target, send_sem, own=False):
        there = keys.at[block, piece_of(piece), :]
        return pltpu.make_async_remote_copy(
            src_ref=latents.at[piece_of(piece), :] if own else there,
            dst_ref=there,
            send_sem=send_sem,
            recv_sem=recv_sem.at[block, piece],
            device_id={"ctx": target},
            device_id_type=MESH,
        )

    twin = place(z, x, 1 - core)
    above = place(lax.rem(z + 1, deep), x, core)
    below = place(lax.rem(z + deep - 1, deep), x, core)
    sides = [lax.rem(x + d, wide) for d in range(1, wide)]

    groups = uk_sem.shape[0]
    per = heads // groups
    raw_copy = pltpu.make_async_copy(queries, raw, local_sem.at[0])
    raw_copy.start()
    uk_copies = []
    for g in range(groups):
        part = pl.ds(g * per, per)
        uk_copies.append(pltpu.make_async_copy(w_uk.at[part], uk.at[part], uk_sem.at[g]))
        uk_copies[-1].start()
    own_copy = pltpu.make_async_copy(latents, keys.at[index], local_sem.at[1])
    own_copy.start()

    barrier = pltpu.get_barrier_semaphore()

    def greet(target):
        pl.semaphore_signal(barrier, inc=1, device_id={"ctx": target}, device_id_type=MESH)

    greet(twin)
    for side in sides:
        greet(place(z, side, core))

    @pl.when(z + 1 < deep)
    def _():
        greet(above)

    @pl.when(z > 0)
    def _():
        greet(below)

    ends = (z + 1 < deep).astype(jnp.int32) + (z > 0).astype(jnp.int32)
    pl.semaphore_wait(barrier, wide + ends)

    def spread(step, piece, own, act):
        block = place(z - step, x, core)

        @pl.when(z + 1 < deep)
        def _():
            act(copy(block, piece, above, up_sem.at[step, piece], own))

        for d, side in enumerate(sides):
            def to_side():
                act(copy(block, piece, place(z, side, core), side_sem.at[step, d, piece], own))

            if own:
                pl.when(side > x)(to_side)
            else:
                to_side()
        act(copy(block, piece, twin, twin_sem.at[step, piece], own))

    def arrived(block, piece):
        copy(block, piece, twin, twin_sem.at[0, 0]).wait_recv()

    def whole(block):
        for piece in range(PIECES):
            arrived(block, piece)

    def needed(step, side):
        return jnp.logical_or(step >= 1, side < x)

    def column(step, piece):
        arrived(place(z - step, x, core), piece)
        spread(step, piece, False, lambda c: c.start())

    def across(step, piece):
        for d, side in enumerate(sides):
            @pl.when(needed(step, side))
            def _():
                block = place(z - step, side, core)
                arrived(block, piece)
                copy(block, piece, twin, pass_sem.at[step, d, piece]).start()

    for piece in range(PIECES):
        spread(0, piece, True, lambda c: c.start())

    raw_copy.wait()
    uv_copy = pltpu.make_async_copy(w_uv, uv, local_sem.at[2])
    for h in range(heads):
        if h % per == 0:
            uk_copies[h // per].wait()
        query = raw[:, h * width:(h + 1) * width]
        lat = jnp.dot(query[:, :nope], uk[h], preferred_element_type=jnp.float32)
        q_all[h * rows:(h + 1) * rows, :rank] = lat.astype(jnp.bfloat16)
        q_all[h * rows:(h + 1) * rows, rank:] = query[:, nope:]
    uv_copy.start()

    parts = 2
    high = heads * rows // parts

    def attend(pair, first):
        blocks = [keys[pair * CORES + c] for c in range(CORES)]
        key = jnp.concatenate(blocks, axis=1)
        value = key[:rank, :].T
        owns = [pl.ds(part * high, high) for part in range(parts)]
        scores = [
            jnp.dot(q_all[own, :], key, preferred_element_type=jnp.float32) for own in owns
        ]
        for own, score in zip(owns, scores):
            if first:
                row = lax.broadcasted_iota(jnp.int32, score.shape, 0)
                col = lax.broadcasted_iota(jnp.int32, score.shape, 1)
                limit = core * krows + krows - rows + lax.rem(row, rows)
                score = jnp.where(col <= limit, score, -jnp.inf)
            best = jnp.max(score, axis=1, keepdims=True)
            if not first:
                old = top[own, :1]
                best = jnp.maximum(old, best)
            expo = jnp.exp2((score - best) * factor)
            lanes = expo[:, :128]
            for lane in range(128, span, 128):
                lanes = lanes + expo[:, lane:lane + 128]
            gain = jnp.dot(expo.astype(jnp.bfloat16), value, preferred_element_type=jnp.float32)
            if first:
                total[own, :] = lanes
                acc[own, :] = gain
            else:
                shrink = jnp.exp2((old - best) * factor)
                total[own, :] = total[own, :] * shrink + lanes
                acc[own, :] = acc[own, :] * shrink + gain
            top[own, :] = jnp.broadcast_to(best, (high, 128))

    def attend_column(step):
        whole(place(z - step, x, 1 - core))
        attend((z - step) * wide + x, False)

    def attend_across(step):
        for side in sides:
            @pl.when(needed(step, side))
            def _():
                whole(place(z - step, side, 1 - core))
                attend((z - step) * wide + side, False)

    own_copy.wait()
    whole(twin)
    attend(index // CORES, True)

    def step_of(step, carry):
        column(step, 0)
        across(step - 1, 0)

        @pl.when(step >= 2)
        def _():
            attend_column(step - 1)

        for piece in range(1, PIECES):
            column(step, piece)
            across(step - 1, piece)

        @pl.when(step >= 2)
        def _():
            attend_across(step - 2)

        return carry

    lax.fori_loop(1, z + 1, step_of, 0)
    across(z, 0)

    @pl.when(z >= 1)
    def _():
        attend_column(z)
        attend_across(z - 1)

    for piece in range(1, PIECES):
        across(z, piece)
    attend_across(z)

    uv_copy.wait()
    for h in range(heads):
        own = pl.ds(h * rows, rows)
        mass = jnp.sum(total[own, :], axis=1, keepdims=True)
        mixed = (acc[own, :] * (1.0 / mass)).astype(jnp.bfloat16)
        out[:, h * vdim:(h + 1) * vdim] = jnp.dot(
            mixed, uv[h], preferred_element_type=jnp.float32
        ).astype(out.dtype)

    def drain(step, carry):
        for piece in range(PIECES):
            @pl.when(step >= 1)
            def _():
                spread(step, piece, False, lambda c: c.wait_send())

            for d, side in enumerate(sides):
                @pl.when(needed(step, side))
                def _():
                    block = place(z - step, side, core)
                    copy(block, piece, twin, pass_sem.at[step, d, piece]).wait_send()
        return carry

    for piece in range(PIECES):
        spread(0, piece, True, lambda c: c.wait_send())
    lax.fori_loop(0, z + 1, drain, 0)


def body(count, queries, latents, w_uk, w_uv):
    deep, wide = grid_of(count)
    heads, nope, rank = w_uk.shape
    vdim = w_uv.shape[2]
    rows = queries.shape[0]
    krows, width = latents.shape
    dma = pltpu.SemaphoreType.DMA
    lanes = max(wide - 1, 1)
    return pl.pallas_call(
        functools.partial(kernel, deep, wide, heads, nope, rank),
        out_shape=jax.ShapeDtypeStruct((rows, heads * vdim), jnp.bfloat16),
        in_specs=[pl.BlockSpec(memory_space=pltpu.HBM)] * 4,
        out_specs=pl.BlockSpec(memory_space=pltpu.VMEM),
        scratch_shapes=[
            pltpu.VMEM((count, width, krows), jnp.bfloat16),
            pltpu.VMEM(queries.shape, jnp.bfloat16),
            pltpu.VMEM((heads * rows, width), jnp.bfloat16),
            pltpu.VMEM(w_uk.shape, jnp.bfloat16),
            pltpu.VMEM(w_uv.shape, jnp.bfloat16),
            pltpu.VMEM((heads * rows, 128), jnp.float32),
            pltpu.VMEM((heads * rows, 128), jnp.float32),
            pltpu.VMEM((heads * rows, rank), jnp.float32),
            dma((deep, PIECES)),
            dma((deep, lanes, PIECES)),
            dma((deep, PIECES)),
            dma((deep, lanes, PIECES)),
            dma((count, PIECES)),
            dma((3,)),
            dma((4,)),
        ],
        compiler_params=pltpu.CompilerParams(
            collective_id=0, has_side_effects=True, vmem_limit_bytes=60 * 1024 * 1024
        ),
    )(queries, latents.T, w_uk, w_uv)


def solution(mesh):
    placed = (P(("groups", "ctx"), None), P(("groups", "ctx"), None), P(), P())
    return jax.shard_map(
        functools.partial(body, mesh.shape["ctx"]),
        mesh=mesh, in_specs=placed, out_specs=P(("groups", "ctx"), None), check_vma=False,
    )
```

```python
import functools
import math

import jax
import jax.numpy as jnp
from jax import lax
from jax.experimental import pallas as pl
from jax.experimental.pallas import tpu as pltpu
from jax.sharding import PartitionSpec as P

CORES = 2
PIECES = 4
MESH = pl.DeviceIdType.MESH


def grid_of(count):
    chips = count // CORES
    wide = 1 << (int(math.log2(chips)) // 3)
    return chips // wide, wide


def kernel(
    deep, wide, heads, nope, rank,
    queries, latents, w_uk, w_uv, out,
    keys, raw, q_all, uk, uv, top, total, acc,
    up_sem, side_sem, twin_sem, pass_sem, recv_sem, local_sem, uk_sem,
):
    index = lax.axis_index("ctx")
    core = lax.rem(index, CORES)
    x = lax.rem(index // CORES, wide)
    z = index // (CORES * wide)
    rows = out.shape[0]
    krows = latents.shape[1]
    width = raw.shape[1] // heads
    vdim = out.shape[1] // heads
    span = CORES * krows
    factor = math.log2(math.e) / math.sqrt(width)

    def place(zz, xx, cc):
        return (zz * wide + xx) * CORES + cc

    def piece_of(piece):
        size = keys.shape[1] // PIECES
        return pl.ds(piece * size, size)

    def copy(block, piece, target, send_sem, own=False):
        there = keys.at[block, piece_of(piece), :]
        return pltpu.make_async_remote_copy(
            src_ref=latents.at[piece_of(piece), :] if own else there,
            dst_ref=there,
            send_sem=send_sem,
            recv_sem=recv_sem.at[block, piece],
            device_id={"ctx": target},
            device_id_type=MESH,
        )

    twin = place(z, x, 1 - core)
    above = place(lax.rem(z + 1, deep), x, core)
    below = place(lax.rem(z + deep - 1, deep), x, core)
    sides = [lax.rem(x + d, wide) for d in range(1, wide)]

    groups = uk_sem.shape[0]
    per = heads // groups
    raw_copy = pltpu.make_async_copy(queries, raw, local_sem.at[0])
    raw_copy.start()
    uk_copies = []
    for g in range(groups):
        part = pl.ds(g * per, per)
        uk_copies.append(pltpu.make_async_copy(w_uk.at[part], uk.at[part], uk_sem.at[g]))
        uk_copies[-1].start()
    own_copy = pltpu.make_async_copy(latents, keys.at[index], local_sem.at[1])
    own_copy.start()

    barrier = pltpu.get_barrier_semaphore()

    def greet(target):
        pl.semaphore_signal(barrier, inc=1, device_id={"ctx": target}, device_id_type=MESH)

    greet(twin)
    for side in sides:
        greet(place(z, side, core))

    @pl.when(z + 1 < deep)
    def _():
        greet(above)

    @pl.when(z > 0)
    def _():
        greet(below)

    ends = (z + 1 < deep).astype(jnp.int32) + (z > 0).astype(jnp.int32)
    pl.semaphore_wait(barrier, wide + ends)

    def spread(step, piece, own, act):
        block = place(z - step, x, core)

        @pl.when(z + 1 < deep)
        def _():
            act(copy(block, piece, above, up_sem.at[step, piece], own))

        for d, side in enumerate(sides):
            def to_side():
                act(copy(block, piece, place(z, side, core), side_sem.at[step, d, piece], own))

            if own:
                pl.when(side > x)(to_side)
            else:
                to_side()
        act(copy(block, piece, twin, twin_sem.at[step, piece], own))

    def arrived(block, piece):
        copy(block, piece, twin, twin_sem.at[0, 0]).wait_recv()

    def whole(block):
        for piece in range(PIECES):
            arrived(block, piece)

    def needed(step, side):
        return jnp.logical_or(step >= 1, side < x)

    def column(step, piece):
        arrived(place(z - step, x, core), piece)
        spread(step, piece, False, lambda c: c.start())

    def across(step, piece):
        for d, side in enumerate(sides):
            @pl.when(needed(step, side))
            def _():
                block = place(z - step, side, core)
                arrived(block, piece)
                copy(block, piece, twin, pass_sem.at[step, d, piece]).start()

    for piece in range(PIECES):
        spread(0, piece, True, lambda c: c.start())

    raw_copy.wait()
    uv_copy = pltpu.make_async_copy(w_uv, uv, local_sem.at[2])
    for h in range(heads):
        if h % per == 0:
            uk_copies[h // per].wait()
        query = raw[:, h * width:(h + 1) * width]
        lat = jnp.dot(query[:, :nope], uk[h], preferred_element_type=jnp.float32)
        q_all[h * rows:(h + 1) * rows, :rank] = lat.astype(jnp.bfloat16)
        q_all[h * rows:(h + 1) * rows, rank:] = query[:, nope:]
    uv_copy.start()

    parts = 2
    high = heads * rows // parts

    def attend(pair, first):
        blocks = [keys[pair * CORES + c] for c in range(CORES)]
        key = jnp.concatenate(blocks, axis=1)
        value = key[:rank, :].T
        owns = [pl.ds(part * high, high) for part in range(parts)]
        scores = [
            jnp.dot(q_all[own, :], key, preferred_element_type=jnp.float32) for own in owns
        ]
        for own, score in zip(owns, scores):
            if first:
                row = lax.broadcasted_iota(jnp.int32, score.shape, 0)
                col = lax.broadcasted_iota(jnp.int32, score.shape, 1)
                limit = core * krows + krows - rows + lax.rem(row, rows)
                score = jnp.where(col <= limit, score, -jnp.inf)
            best = jnp.max(score, axis=1, keepdims=True)
            if not first:
                old = top[own, :1]
                best = jnp.maximum(old, best)
            expo = jnp.exp2((score - best) * factor)
            lanes = expo[:, :128]
            for lane in range(128, span, 128):
                lanes = lanes + expo[:, lane:lane + 128]
            gain = jnp.dot(expo.astype(jnp.bfloat16), value, preferred_element_type=jnp.float32)
            if first:
                total[own, :] = lanes
                acc[own, :] = gain
            else:
                shrink = jnp.exp2((old - best) * factor)
                total[own, :] = total[own, :] * shrink + lanes
                acc[own, :] = acc[own, :] * shrink + gain
            top[own, :] = jnp.broadcast_to(best, (high, 128))

    def attend_column(step):
        whole(place(z - step, x, 1 - core))
        attend((z - step) * wide + x, False)

    def attend_across(step):
        for side in sides:
            @pl.when(needed(step, side))
            def _():
                whole(place(z - step, side, 1 - core))
                attend((z - step) * wide + side, False)

    own_copy.wait()
    whole(twin)
    attend(index // CORES, True)

    def step_of(step, carry):
        for piece in range(PIECES // 2):
            column(step, piece)
            across(step - 1, piece)

        @pl.when(step >= 2)
        def _():
            attend_column(step - 1)

        for piece in range(PIECES // 2, PIECES):
            column(step, piece)
            across(step - 1, piece)

        @pl.when(step >= 2)
        def _():
            attend_across(step - 2)

        return carry

    lax.fori_loop(1, z + 1, step_of, 0)
    for piece in range(PIECES // 2):
        across(z, piece)

    @pl.when(z >= 1)
    def _():
        attend_column(z)
        attend_across(z - 1)

    for piece in range(PIECES // 2, PIECES):
        across(z, piece)
    attend_across(z)

    uv_copy.wait()
    for h in range(heads):
        own = pl.ds(h * rows, rows)
        mass = jnp.sum(total[own, :], axis=1, keepdims=True)
        mixed = (acc[own, :] * (1.0 / mass)).astype(jnp.bfloat16)
        out[:, h * vdim:(h + 1) * vdim] = jnp.dot(
            mixed, uv[h], preferred_element_type=jnp.float32
        ).astype(out.dtype)

    def drain(step, carry):
        for piece in range(PIECES):
            @pl.when(step >= 1)
            def _():
                spread(step, piece, False, lambda c: c.wait_send())

            for d, side in enumerate(sides):
                @pl.when(needed(step, side))
                def _():
                    block = place(z - step, side, core)
                    copy(block, piece, twin, pass_sem.at[step, d, piece]).wait_send()
        return carry

    for piece in range(PIECES):
        spread(0, piece, True, lambda c: c.wait_send())
    lax.fori_loop(0, z + 1, drain, 0)


def body(count, queries, latents, w_uk, w_uv):
    deep, wide = grid_of(count)
    heads, nope, rank = w_uk.shape
    vdim = w_uv.shape[2]
    rows = queries.shape[0]
    krows, width = latents.shape
    dma = pltpu.SemaphoreType.DMA
    lanes = max(wide - 1, 1)
    return pl.pallas_call(
        functools.partial(kernel, deep, wide, heads, nope, rank),
        out_shape=jax.ShapeDtypeStruct((rows, heads * vdim), jnp.bfloat16),
        in_specs=[pl.BlockSpec(memory_space=pltpu.HBM)] * 4,
        out_specs=pl.BlockSpec(memory_space=pltpu.VMEM),
        scratch_shapes=[
            pltpu.VMEM((count, width, krows), jnp.bfloat16),
            pltpu.VMEM(queries.shape, jnp.bfloat16),
            pltpu.VMEM((heads * rows, width), jnp.bfloat16),
            pltpu.VMEM(w_uk.shape, jnp.bfloat16),
            pltpu.VMEM(w_uv.shape, jnp.bfloat16),
            pltpu.VMEM((heads * rows, 128), jnp.float32),
            pltpu.VMEM((heads * rows, 128), jnp.float32),
            pltpu.VMEM((heads * rows, rank), jnp.float32),
            dma((deep, PIECES)),
            dma((deep, lanes, PIECES)),
            dma((deep, PIECES)),
            dma((deep, lanes, PIECES)),
            dma((count, PIECES)),
            dma((3,)),
            dma((4,)),
        ],
        compiler_params=pltpu.CompilerParams(
            collective_id=0, has_side_effects=True, vmem_limit_bytes=55050 * 1024
        ),
    )(queries, latents.T, w_uk, w_uv)


def solution(mesh):
    placed = (P(("groups", "ctx"), None), P(("groups", "ctx"), None), P(), P())
    return jax.shard_map(
        functools.partial(body, mesh.shape["ctx"]),
        mesh=mesh, in_specs=placed, out_specs=P(("groups", "ctx"), None), check_vma=False,
    )
```

```python
import functools
import math

import jax
import jax.numpy as jnp
from jax import lax
from jax.experimental import pallas as pl
from jax.experimental.pallas import tpu as pltpu
from jax.sharding import PartitionSpec as P

CORES = 2
PIECES = 4
HALF = PIECES // 2
MESH = pl.DeviceIdType.MESH


def grid_of(count):
    chips = count // CORES
    wide = 1 << (int(math.log2(chips)) // 3)
    return chips // wide, wide


def kernel(
    deep, wide, heads, nope, rank,
    queries, latents, w_uk, w_uv, out,
    keys, raw, q_all, uk, uv, top, total, acc,
    up_sem, side_sem, twin_sem, pass_sem, far_sem, recv_sem, local_sem, uk_sem,
):
    index = lax.axis_index("ctx")
    core = lax.rem(index, CORES)
    x = lax.rem(index // CORES, wide)
    z = index // (CORES * wide)
    rows = out.shape[0]
    krows = latents.shape[1]
    width = raw.shape[1] // heads
    vdim = out.shape[1] // heads
    span = CORES * krows
    factor = math.log2(math.e) / math.sqrt(width)

    def place(zz, xx, cc):
        return (zz * wide + xx) * CORES + cc

    def piece_of(piece):
        size = keys.shape[1] // PIECES
        return pl.ds(piece * size, size)

    def copy(block, piece, target, send_sem, own=False):
        there = keys.at[block, piece_of(piece), :]
        return pltpu.make_async_remote_copy(
            src_ref=latents.at[piece_of(piece), :] if own else there,
            dst_ref=there,
            send_sem=send_sem,
            recv_sem=recv_sem.at[block, piece],
            device_id={"ctx": target},
            device_id_type=MESH,
        )

    twin = place(z, x, 1 - core)
    above = place(lax.rem(z + 1, deep), x, core)
    below = place(lax.rem(z + deep - 1, deep), x, core)
    sides = [lax.rem(x + d, wide) for d in range(1, wide)]

    groups = uk_sem.shape[0]
    per = heads // groups
    raw_copy = pltpu.make_async_copy(queries, raw, local_sem.at[0])
    raw_copy.start()
    uk_copies = []
    for g in range(groups):
        part = pl.ds(g * per, per)
        uk_copies.append(pltpu.make_async_copy(w_uk.at[part], uk.at[part], uk_sem.at[g]))
        uk_copies[-1].start()
    own_copy = pltpu.make_async_copy(latents, keys.at[index], local_sem.at[1])
    own_copy.start()

    barrier = pltpu.get_barrier_semaphore()

    def greet(target):
        pl.semaphore_signal(barrier, inc=1, device_id={"ctx": target}, device_id_type=MESH)

    greet(twin)
    for side in sides:
        greet(place(z, side, core))

    @pl.when(z + 1 < deep)
    def _():
        greet(above)

    @pl.when(z > 0)
    def _():
        greet(below)

    ends = (z + 1 < deep).astype(jnp.int32) + (z > 0).astype(jnp.int32)
    pl.semaphore_wait(barrier, wide + ends)

    def spread(step, piece, own, act):
        block = place(z - step, x, core)

        @pl.when(z + 1 < deep)
        def _():
            act(copy(block, piece, above, up_sem.at[step, piece], own))

        for d, side in enumerate(sides):
            def to_side():
                act(copy(block, piece, place(z, side, core), side_sem.at[step, d, piece], own))

            if own and piece >= HALF:
                pl.when(jnp.logical_or(side > x, z == 0))(to_side)
            elif own:
                pl.when(side > x)(to_side)
            elif piece >= HALF:
                pl.when(step < z)(to_side)
            else:
                to_side()
        act(copy(block, piece, twin, twin_sem.at[step, piece], own))

    def arrived(block, piece):
        copy(block, piece, twin, twin_sem.at[0, 0]).wait_recv()

    def whole(block):
        for piece in range(PIECES):
            arrived(block, piece)

    def needed(step, side):
        return jnp.logical_or(step >= 1, side < x)

    def column(step, piece):
        arrived(place(z - step, x, core), piece)
        spread(step, piece, False, lambda c: c.start())

    def hand(step, piece, d, side, act):
        act(copy(place(z - step, side, core), piece, twin, pass_sem.at[step, d, piece]))

    def relay(piece, d, side, act):
        @pl.when(z + 1 < deep)
        def _():
            act(copy(place(0, side, core), piece, above, far_sem.at[d, piece]))

    def across(step, piece):
        for d, side in enumerate(sides):
            @pl.when(needed(step, side))
            def _():
                arrived(place(z - step, side, core), piece)
                hand(step, piece, d, side, lambda c: c.start())

    def far(piece):
        for d, side in enumerate(sides):
            arrived(place(0, side, core), piece)
            relay(piece, d, side, lambda c: c.start())

            @pl.when(needed(z, side))
            def _():
                hand(z, piece, d, side, lambda c: c.start())

    for piece in range(PIECES):
        spread(0, piece, True, lambda c: c.start())

    raw_copy.wait()
    uv_copy = pltpu.make_async_copy(w_uv, uv, local_sem.at[2])
    for h in range(heads):
        if h % per == 0:
            uk_copies[h // per].wait()
        query = raw[:, h * width:(h + 1) * width]
        lat = jnp.dot(query[:, :nope], uk[h], preferred_element_type=jnp.float32)
        q_all[h * rows:(h + 1) * rows, :rank] = lat.astype(jnp.bfloat16)
        q_all[h * rows:(h + 1) * rows, rank:] = query[:, nope:]
    uv_copy.start()

    parts = 2
    high = heads * rows // parts

    def attend(pair, first):
        blocks = [keys[pair * CORES + c] for c in range(CORES)]
        key = jnp.concatenate(blocks, axis=1)
        value = key[:rank, :].T
        owns = [pl.ds(part * high, high) for part in range(parts)]
        scores = [
            jnp.dot(q_all[own, :], key, preferred_element_type=jnp.float32) for own in owns
        ]
        for own, score in zip(owns, scores):
            if first:
                row = lax.broadcasted_iota(jnp.int32, score.shape, 0)
                col = lax.broadcasted_iota(jnp.int32, score.shape, 1)
                limit = core * krows + krows - rows + lax.rem(row, rows)
                score = jnp.where(col <= limit, score, -jnp.inf)
            best = jnp.max(score, axis=1, keepdims=True)
            if not first:
                old = top[own, :1]
                best = jnp.maximum(old, best)
            expo = jnp.exp2((score - best) * factor)
            lanes = expo[:, :128]
            for lane in range(128, span, 128):
                lanes = lanes + expo[:, lane:lane + 128]
            gain = jnp.dot(expo.astype(jnp.bfloat16), value, preferred_element_type=jnp.float32)
            if first:
                total[own, :] = lanes
                acc[own, :] = gain
            else:
                shrink = jnp.exp2((old - best) * factor)
                total[own, :] = total[own, :] * shrink + lanes
                acc[own, :] = acc[own, :] * shrink + gain
            top[own, :] = jnp.broadcast_to(best, (high, 128))

    def attend_column(step):
        whole(place(z - step, x, 1 - core))
        attend((z - step) * wide + x, False)

    def attend_across(step):
        for side in sides:
            @pl.when(needed(step, side))
            def _():
                whole(place(z - step, side, 1 - core))
                attend((z - step) * wide + side, False)

    own_copy.wait()
    whole(twin)
    attend(index // CORES, True)

    low, up = range(HALF), range(HALF, PIECES)

    def step_of(step, carry):
        for piece in low:
            column(step, piece)

        @pl.when(step >= 2)
        def _():
            for piece in up:
                across(step - 2, piece)
            attend_column(step - 1)

        for piece in up:
            column(step, piece)
        for piece in low:
            across(step - 1, piece)

        @pl.when(step >= 2)
        def _():
            attend_across(step - 2)

        return carry

    lax.fori_loop(1, z + 1, step_of, 0)

    @pl.when(z >= 1)
    def _():
        for piece in up:
            across(z - 1, piece)
        attend_column(z)

    for piece in low:
        across(z, piece)
    for piece in up:
        far(piece)

    @pl.when(z >= 1)
    def _():
        attend_across(z - 1)

    attend_across(z)

    uv_copy.wait()
    for h in range(heads):
        own = pl.ds(h * rows, rows)
        mass = jnp.sum(total[own, :], axis=1, keepdims=True)
        mixed = (acc[own, :] * (1.0 / mass)).astype(jnp.bfloat16)
        out[:, h * vdim:(h + 1) * vdim] = jnp.dot(
            mixed, uv[h], preferred_element_type=jnp.float32
        ).astype(out.dtype)

    def drain(step, carry):
        for piece in range(PIECES):
            @pl.when(step >= 1)
            def _():
                spread(step, piece, False, lambda c: c.wait_send())

            for d, side in enumerate(sides):
                @pl.when(needed(step, side))
                def _():
                    hand(step, piece, d, side, lambda c: c.wait_send())
        return carry

    for piece in range(PIECES):
        spread(0, piece, True, lambda c: c.wait_send())
    lax.fori_loop(0, z + 1, drain, 0)
    for piece in up:
        for d, side in enumerate(sides):
            relay(piece, d, side, lambda c: c.wait_send())


def body(count, queries, latents, w_uk, w_uv):
    deep, wide = grid_of(count)
    heads, nope, rank = w_uk.shape
    vdim = w_uv.shape[2]
    rows = queries.shape[0]
    krows, width = latents.shape
    dma = pltpu.SemaphoreType.DMA
    lanes = max(wide - 1, 1)
    return pl.pallas_call(
        functools.partial(kernel, deep, wide, heads, nope, rank),
        out_shape=jax.ShapeDtypeStruct((rows, heads * vdim), jnp.bfloat16),
        in_specs=[pl.BlockSpec(memory_space=pltpu.HBM)] * 4,
        out_specs=pl.BlockSpec(memory_space=pltpu.VMEM),
        scratch_shapes=[
            pltpu.VMEM((count, width, krows), jnp.bfloat16),
            pltpu.VMEM(queries.shape, jnp.bfloat16),
            pltpu.VMEM((heads * rows, width), jnp.bfloat16),
            pltpu.VMEM(w_uk.shape, jnp.bfloat16),
            pltpu.VMEM(w_uv.shape, jnp.bfloat16),
            pltpu.VMEM((heads * rows, 128), jnp.float32),
            pltpu.VMEM((heads * rows, 128), jnp.float32),
            pltpu.VMEM((heads * rows, rank), jnp.float32),
            dma((deep, PIECES)),
            dma((deep, lanes, PIECES)),
            dma((deep, PIECES)),
            dma((deep, lanes, PIECES)),
            dma((lanes, PIECES)),
            dma((count, PIECES)),
            dma((3,)),
            dma((4,)),
        ],
        compiler_params=pltpu.CompilerParams(
            collective_id=0, has_side_effects=True, vmem_limit_bytes=55050 * 1024
        ),
    )(queries, latents.T, w_uk, w_uv)


def solution(mesh):
    placed = (P(("groups", "ctx"), None), P(("groups", "ctx"), None), P(), P())
    return jax.shard_map(
        functools.partial(body, mesh.shape["ctx"]),
        mesh=mesh, in_specs=placed, out_specs=P(("groups", "ctx"), None), check_vma=False,
    )
```

```python
import functools
import math

import jax
import jax.numpy as jnp
from jax import lax
from jax.experimental import pallas as pl
from jax.experimental.pallas import tpu as pltpu
from jax.sharding import PartitionSpec as P

CORES = 2
PIECES = 4
HALF = PIECES // 2
LAST = PIECES - 1
MESH = pl.DeviceIdType.MESH


def grid_of(count):
    chips = count // CORES
    wide = 1 << (int(math.log2(chips)) // 3)
    return chips // wide, wide


def kernel(
    deep, wide, heads, nope, rank,
    queries, latents, w_uk, w_uv, out,
    keys, raw, q_all, uk, uv, top, total, acc,
    up_sem, side_sem, twin_sem, pass_sem, far_sem, recv_sem, local_sem, uk_sem,
):
    index = lax.axis_index("ctx")
    core = lax.rem(index, CORES)
    x = lax.rem(index // CORES, wide)
    z = index // (CORES * wide)
    rows = out.shape[0]
    krows = latents.shape[1]
    width = raw.shape[1] // heads
    vdim = out.shape[1] // heads
    span = CORES * krows
    factor = math.log2(math.e) / math.sqrt(width)

    def place(zz, xx, cc):
        return (zz * wide + xx) * CORES + cc

    def piece_of(piece):
        size = keys.shape[1] // PIECES
        return pl.ds(piece * size, size)

    def copy(block, piece, target, send_sem, own=False):
        there = keys.at[block, piece_of(piece), :]
        return pltpu.make_async_remote_copy(
            src_ref=latents.at[piece_of(piece), :] if own else there,
            dst_ref=there,
            send_sem=send_sem,
            recv_sem=recv_sem.at[block, piece],
            device_id={"ctx": target},
            device_id_type=MESH,
        )

    twin = place(z, x, 1 - core)
    above = place(lax.rem(z + 1, deep), x, core)
    below = place(lax.rem(z + deep - 1, deep), x, core)
    sides = [lax.rem(x + d, wide) for d in range(1, wide)]

    barrier = pltpu.get_barrier_semaphore()

    def greet(target):
        pl.semaphore_signal(barrier, inc=1, device_id={"ctx": target}, device_id_type=MESH)

    greet(twin)
    for side in sides:
        greet(place(z, side, core))

    @pl.when(z + 1 < deep)
    def _():
        greet(above)

    @pl.when(z > 0)
    def _():
        greet(below)

    groups = uk_sem.shape[0]
    per = heads // groups
    raw_copy = pltpu.make_async_copy(queries, raw, local_sem.at[0])
    raw_copy.start()
    uk_copies = []
    for g in range(groups):
        part = pl.ds(g * per, per)
        uk_copies.append(pltpu.make_async_copy(w_uk.at[part], uk.at[part], uk_sem.at[g]))
        uk_copies[-1].start()
    own_copy = pltpu.make_async_copy(latents, keys.at[index], local_sem.at[1])
    own_copy.start()

    ends = (z + 1 < deep).astype(jnp.int32) + (z > 0).astype(jnp.int32)
    pl.semaphore_wait(barrier, wide + ends)

    def spread(step, piece, own, act):
        block = place(z - step, x, core)

        @pl.when(z + 1 < deep)
        def _():
            act(copy(block, piece, above, up_sem.at[step, piece], own))

        for d, side in enumerate(sides):
            def to_side():
                act(copy(block, piece, place(z, side, core), side_sem.at[step, d, piece], own))

            if own and piece >= LAST:
                pl.when(jnp.logical_or(side > x, z == 0))(to_side)
            elif own:
                pl.when(side > x)(to_side)
            elif piece >= LAST:
                pl.when(step < z)(to_side)
            elif piece >= HALF:
                pl.when(jnp.logical_or(step < z, side < x))(to_side)
            else:
                to_side()
        act(copy(block, piece, twin, twin_sem.at[step, piece], own))

    def arrived(block, piece):
        copy(block, piece, twin, twin_sem.at[0, 0]).wait_recv()

    def whole(block):
        for piece in range(PIECES):
            arrived(block, piece)

    def needed(step, side):
        return jnp.logical_or(step >= 1, side < x)

    def column(step, piece):
        arrived(place(z - step, x, core), piece)
        spread(step, piece, False, lambda c: c.start())

    def hand(step, piece, d, side, act):
        act(copy(place(z - step, side, core), piece, twin, pass_sem.at[step, d, piece]))

    def by_column(piece, side):
        return jnp.logical_or(side < x, piece >= LAST)

    def relay(piece, d, side, act):
        @pl.when(jnp.logical_and(by_column(piece, side), z + 1 < deep))
        def _():
            act(copy(place(0, side, core), piece, above, far_sem.at[d, piece]))

    def across(step, piece):
        for d, side in enumerate(sides):
            @pl.when(needed(step, side))
            def _():
                arrived(place(z - step, side, core), piece)
                hand(step, piece, d, side, lambda c: c.start())

    def far(piece):
        for d, side in enumerate(sides):
            @pl.when(jnp.logical_or(by_column(piece, side), needed(z, side)))
            def _():
                arrived(place(0, side, core), piece)

            relay(piece, d, side, lambda c: c.start())

            @pl.when(needed(z, side))
            def _():
                hand(z, piece, d, side, lambda c: c.start())

    for piece in range(PIECES):
        spread(0, piece, True, lambda c: c.start())

    raw_copy.wait()
    uv_copy = pltpu.make_async_copy(w_uv, uv, local_sem.at[2])
    for h in range(heads):
        if h % per == 0:
            uk_copies[h // per].wait()
        query = raw[:, h * width:(h + 1) * width]
        lat = jnp.dot(query[:, :nope], uk[h], preferred_element_type=jnp.float32)
        q_all[h * rows:(h + 1) * rows, :rank] = lat.astype(jnp.bfloat16)
        q_all[h * rows:(h + 1) * rows, rank:] = query[:, nope:]
    uv_copy.start()

    parts = 2
    high = heads * rows // parts

    def attend(pair, first):
        blocks = [keys[pair * CORES + c] for c in range(CORES)]
        key = jnp.concatenate(blocks, axis=1)
        value = key[:rank, :].T
        owns = [pl.ds(part * high, high) for part in range(parts)]
        scores = [
            jnp.dot(q_all[own, :], key, preferred_element_type=jnp.float32) for own in owns
        ]
        for own, score in zip(owns, scores):
            if first:
                row = lax.broadcasted_iota(jnp.int32, score.shape, 0)
                col = lax.broadcasted_iota(jnp.int32, score.shape, 1)
                limit = core * krows + krows - rows + lax.rem(row, rows)
                score = jnp.where(col <= limit, score, -jnp.inf)
            best = jnp.max(score, axis=1, keepdims=True)
            if not first:
                old = top[own, :1]
                best = jnp.maximum(old, best)
            expo = jnp.exp2((score - best) * factor)
            lanes = expo[:, :128]
            for lane in range(128, span, 128):
                lanes = lanes + expo[:, lane:lane + 128]
            gain = jnp.dot(expo.astype(jnp.bfloat16), value, preferred_element_type=jnp.float32)
            if first:
                total[own, :] = lanes
                acc[own, :] = gain
            else:
                shrink = jnp.exp2((old - best) * factor)
                total[own, :] = total[own, :] * shrink + lanes
                acc[own, :] = acc[own, :] * shrink + gain
            top[own, :] = jnp.broadcast_to(best, (high, 128))

    def attend_column(step):
        whole(place(z - step, x, 1 - core))
        attend((z - step) * wide + x, False)

    def attend_across(step):
        for side in sides:
            @pl.when(needed(step, side))
            def _():
                whole(place(z - step, side, 1 - core))
                attend((z - step) * wide + side, False)

    own_copy.wait()
    whole(twin)
    attend(index // CORES, True)

    low, up = range(HALF), range(HALF, PIECES)

    def step_of(step, carry):
        for piece in low:
            column(step, piece)

        @pl.when(step >= 2)
        def _():
            for piece in up:
                across(step - 2, piece)
            attend_column(step - 1)

        for piece in up:
            column(step, piece)
        for piece in low:
            across(step - 1, piece)

        @pl.when(step >= 2)
        def _():
            attend_across(step - 2)

        return carry

    lax.fori_loop(1, z + 1, step_of, 0)

    @pl.when(z >= 1)
    def _():
        for piece in up:
            across(z - 1, piece)
        attend_column(z)

    for piece in range(HALF):
        across(z, piece)
        far(HALF + piece)
        if piece == 0:
            @pl.when(z >= 1)
            def _():
                attend_across(z - 1)

    attend_across(z)

    uv_copy.wait()
    for h in range(heads):
        own = pl.ds(h * rows, rows)
        mass = jnp.sum(total[own, :], axis=1, keepdims=True)
        mixed = (acc[own, :] * (1.0 / mass)).astype(jnp.bfloat16)
        out[:, h * vdim:(h + 1) * vdim] = jnp.dot(
            mixed, uv[h], preferred_element_type=jnp.float32
        ).astype(out.dtype)

    def drain(step, carry):
        for piece in range(PIECES):
            @pl.when(step >= 1)
            def _():
                spread(step, piece, False, lambda c: c.wait_send())

            for d, side in enumerate(sides):
                @pl.when(needed(step, side))
                def _():
                    hand(step, piece, d, side, lambda c: c.wait_send())
        return carry

    for piece in range(PIECES):
        spread(0, piece, True, lambda c: c.wait_send())
    lax.fori_loop(0, z + 1, drain, 0)
    for piece in up:
        for d, side in enumerate(sides):
            relay(piece, d, side, lambda c: c.wait_send())


def body(count, queries, latents, w_uk, w_uv):
    deep, wide = grid_of(count)
    heads, nope, rank = w_uk.shape
    vdim = w_uv.shape[2]
    rows = queries.shape[0]
    krows, width = latents.shape
    dma = pltpu.SemaphoreType.DMA
    lanes = max(wide - 1, 1)
    return pl.pallas_call(
        functools.partial(kernel, deep, wide, heads, nope, rank),
        out_shape=jax.ShapeDtypeStruct((rows, heads * vdim), jnp.bfloat16),
        in_specs=[pl.BlockSpec(memory_space=pltpu.HBM)] * 4,
        out_specs=pl.BlockSpec(memory_space=pltpu.VMEM),
        scratch_shapes=[
            pltpu.VMEM((count, width, krows), jnp.bfloat16),
            pltpu.VMEM(queries.shape, jnp.bfloat16),
            pltpu.VMEM((heads * rows, width), jnp.bfloat16),
            pltpu.VMEM(w_uk.shape, jnp.bfloat16),
            pltpu.VMEM(w_uv.shape, jnp.bfloat16),
            pltpu.VMEM((heads * rows, 128), jnp.float32),
            pltpu.VMEM((heads * rows, 128), jnp.float32),
            pltpu.VMEM((heads * rows, rank), jnp.float32),
            dma((deep, PIECES)),
            dma((deep, lanes, PIECES)),
            dma((deep, PIECES)),
            dma((deep, lanes, PIECES)),
            dma((lanes, PIECES)),
            dma((count, PIECES)),
            dma((3,)),
            dma((4,)),
        ],
        compiler_params=pltpu.CompilerParams(
            collective_id=0, has_side_effects=True, vmem_limit_bytes=55050 * 1024
        ),
    )(queries, latents.T, w_uk, w_uv)


def solution(mesh):
    placed = (P(("groups", "ctx"), None), P(("groups", "ctx"), None), P(), P())
    return jax.shard_map(
        functools.partial(body, mesh.shape["ctx"]),
        mesh=mesh, in_specs=placed, out_specs=P(("groups", "ctx"), None), check_vma=False,
    )
```

```python
import functools
import math

import jax
import jax.numpy as jnp
from jax import lax
from jax.experimental import pallas as pl
from jax.experimental.pallas import tpu as pltpu
from jax.sharding import PartitionSpec as P

CORES = 2
PIECES = 4
HALF = PIECES // 2
MESH = pl.DeviceIdType.MESH


def grid_of(count):
    chips = count // CORES
    wide = 1 << (int(math.log2(chips)) // 3)
    return chips // wide, wide


def kernel(
    deep, wide, heads, nope, rank,
    queries, latents, w_uk, w_uv, out,
    keys, raw, q_all, uk, uv, top, total, acc,
    up_sem, side_sem, twin_sem, pass_sem, far_sem, recv_sem, local_sem, uk_sem,
):
    index = lax.axis_index("ctx")
    core = lax.rem(index, CORES)
    x = lax.rem(index // CORES, wide)
    z = index // (CORES * wide)
    rows = out.shape[0]
    krows = latents.shape[1]
    width = raw.shape[1] // heads
    vdim = out.shape[1] // heads
    span = CORES * krows
    factor = math.log2(math.e) / math.sqrt(width)

    def place(zz, xx, cc):
        return (zz * wide + xx) * CORES + cc

    def piece_of(piece):
        size = keys.shape[1] // PIECES
        return pl.ds(piece * size, size)

    def copy(block, piece, target, send_sem, own=False):
        there = keys.at[block, piece_of(piece), :]
        return pltpu.make_async_remote_copy(
            src_ref=latents.at[piece_of(piece), :] if own else there,
            dst_ref=there,
            send_sem=send_sem,
            recv_sem=recv_sem.at[block, piece],
            device_id={"ctx": target},
            device_id_type=MESH,
        )

    twin = place(z, x, 1 - core)
    above = place(lax.rem(z + 1, deep), x, core)
    below = place(lax.rem(z + deep - 1, deep), x, core)
    sides = [lax.rem(x + d, wide) for d in range(1, wide)]

    groups = uk_sem.shape[0]
    per = heads // groups
    raw_copy = pltpu.make_async_copy(queries, raw, local_sem.at[0])
    raw_copy.start()
    uk_copies = []
    for g in range(groups):
        part = pl.ds(g * per, per)
        uk_copies.append(pltpu.make_async_copy(w_uk.at[part], uk.at[part], uk_sem.at[g]))
        uk_copies[-1].start()
    own_copy = pltpu.make_async_copy(latents, keys.at[index], local_sem.at[1])
    own_copy.start()

    barrier = pltpu.get_barrier_semaphore()

    def greet(target):
        pl.semaphore_signal(barrier, inc=1, device_id={"ctx": target}, device_id_type=MESH)

    greet(twin)
    for side in sides:
        greet(place(z, side, core))

    @pl.when(z + 1 < deep)
    def _():
        greet(above)

    @pl.when(z > 0)
    def _():
        greet(below)

    ends = (z + 1 < deep).astype(jnp.int32) + (z > 0).astype(jnp.int32)
    pl.semaphore_wait(barrier, wide + ends)

    def spread(step, piece, own, act):
        block = place(z - step, x, core)

        @pl.when(z + 1 < deep)
        def _():
            act(copy(block, piece, above, up_sem.at[step, piece], own))

        for d, side in enumerate(sides):
            def to_side():
                act(copy(block, piece, place(z, side, core), side_sem.at[step, d, piece], own))

            if own and piece >= HALF:
                pl.when(jnp.logical_or(side > x, z == 0))(to_side)
            elif own:
                pl.when(side > x)(to_side)
            elif piece >= HALF:
                pl.when(step < z)(to_side)
            else:
                to_side()
        act(copy(block, piece, twin, twin_sem.at[step, piece], own))

    def arrived(block, piece):
        copy(block, piece, twin, twin_sem.at[0, 0]).wait_recv()

    def whole(block):
        for piece in range(PIECES):
            arrived(block, piece)

    def needed(step, side):
        return jnp.logical_or(step >= 1, side < x)

    def column(step, piece):
        arrived(place(z - step, x, core), piece)
        spread(step, piece, False, lambda c: c.start())

    def hand(step, piece, d, side, act):
        act(copy(place(z - step, side, core), piece, twin, pass_sem.at[step, d, piece]))

    def relay(piece, d, side, act):
        @pl.when(z + 1 < deep)
        def _():
            act(copy(place(0, side, core), piece, above, far_sem.at[d, piece]))

    def across(step, piece):
        for d, side in enumerate(sides):
            @pl.when(needed(step, side))
            def _():
                arrived(place(z - step, side, core), piece)
                hand(step, piece, d, side, lambda c: c.start())

    def far(piece):
        for d, side in enumerate(sides):
            arrived(place(0, side, core), piece)
            relay(piece, d, side, lambda c: c.start())

            @pl.when(needed(z, side))
            def _():
                hand(z, piece, d, side, lambda c: c.start())

    for piece in range(PIECES):
        spread(0, piece, True, lambda c: c.start())

    raw_copy.wait()
    uv_copy = pltpu.make_async_copy(w_uv, uv, local_sem.at[2])
    for h in range(heads):
        if h % per == 0:
            uk_copies[h // per].wait()
        query = raw[:, h * width:(h + 1) * width]
        lat = jnp.dot(query[:, :nope], uk[h], preferred_element_type=jnp.float32)
        q_all[h * rows:(h + 1) * rows, :rank] = lat.astype(jnp.bfloat16)
        q_all[h * rows:(h + 1) * rows, rank:] = query[:, nope:]
    uv_copy.start()

    parts = 2
    lanes = top.shape[1]
    high = heads * rows // parts

    def attend(pair, first):
        blocks = [keys[pair * CORES + c] for c in range(CORES)]
        key = jnp.concatenate(blocks, axis=1)
        value = key[:rank, :].T
        owns = [pl.ds(part * high, high) for part in range(parts)]
        scores = [
            jnp.dot(q_all[own, :], key, preferred_element_type=jnp.float32) for own in owns
        ]
        for own, score in zip(owns, scores):
            if first:
                row = lax.broadcasted_iota(jnp.int32, score.shape, 0)
                col = lax.broadcasted_iota(jnp.int32, score.shape, 1)
                limit = core * krows + krows - rows + lax.rem(row, rows)
                score = jnp.where(col <= limit, score, -jnp.inf)
            best = jnp.broadcast_to(jnp.max(score, axis=1, keepdims=True), (high, lanes))
            if not first:
                old = top[own, :]
                best = jnp.maximum(old, best)
            expos = [
                jnp.exp2((score[:, lane:lane + lanes] - best) * factor)
                for lane in range(0, span, lanes)
            ]
            mass = functools.reduce(jnp.add, expos)
            weight = jnp.concatenate([e.astype(jnp.bfloat16) for e in expos], axis=1)
            gain = jnp.dot(weight, value, preferred_element_type=jnp.float32)
            if first:
                total[own, :] = mass
                acc[own, :] = gain
            else:
                shrink = jnp.exp2((old - best) * factor)
                total[own, :] = total[own, :] * shrink + mass
                for lane in range(0, rank, lanes):
                    part = slice(lane, lane + lanes)
                    acc[own, part] = acc[own, part] * shrink + gain[:, part]
            top[own, :] = best

    def attend_column(step):
        whole(place(z - step, x, 1 - core))
        attend((z - step) * wide + x, False)

    def attend_across(step):
        for side in sides:
            @pl.when(needed(step, side))
            def _():
                whole(place(z - step, side, 1 - core))
                attend((z - step) * wide + side, False)

    own_copy.wait()
    whole(twin)
    attend(index // CORES, True)

    low, up = range(HALF), range(HALF, PIECES)

    def step_of(step, carry):
        for piece in low:
            column(step, piece)

        @pl.when(step >= 2)
        def _():
            for piece in up:
                across(step - 2, piece)
            attend_column(step - 1)

        for piece in up:
            column(step, piece)
        for piece in low:
            across(step - 1, piece)

        @pl.when(step >= 2)
        def _():
            attend_across(step - 2)

        return carry

    lax.fori_loop(1, z + 1, step_of, 0)

    @pl.when(z >= 1)
    def _():
        for piece in up:
            across(z - 1, piece)
        attend_column(z)

    for piece in low:
        across(z, piece)
    for piece in up:
        far(piece)

    @pl.when(z >= 1)
    def _():
        attend_across(z - 1)

    attend_across(z)

    uv_copy.wait()
    for h in range(heads):
        own = pl.ds(h * rows, rows)
        mass = jnp.sum(total[own, :], axis=1, keepdims=True)
        mixed = (acc[own, :] * (1.0 / mass)).astype(jnp.bfloat16)
        out[:, h * vdim:(h + 1) * vdim] = jnp.dot(
            mixed, uv[h], preferred_element_type=jnp.float32
        ).astype(out.dtype)

    def drain(step, carry):
        for piece in range(PIECES):
            @pl.when(step >= 1)
            def _():
                spread(step, piece, False, lambda c: c.wait_send())

            for d, side in enumerate(sides):
                @pl.when(needed(step, side))
                def _():
                    hand(step, piece, d, side, lambda c: c.wait_send())
        return carry

    for piece in range(PIECES):
        spread(0, piece, True, lambda c: c.wait_send())
    lax.fori_loop(0, z + 1, drain, 0)
    for piece in up:
        for d, side in enumerate(sides):
            relay(piece, d, side, lambda c: c.wait_send())


def body(count, queries, latents, w_uk, w_uv):
    deep, wide = grid_of(count)
    heads, nope, rank = w_uk.shape
    vdim = w_uv.shape[2]
    rows = queries.shape[0]
    krows, width = latents.shape
    dma = pltpu.SemaphoreType.DMA
    lanes = max(wide - 1, 1)
    return pl.pallas_call(
        functools.partial(kernel, deep, wide, heads, nope, rank),
        out_shape=jax.ShapeDtypeStruct((rows, heads * vdim), jnp.bfloat16),
        in_specs=[pl.BlockSpec(memory_space=pltpu.HBM)] * 4,
        out_specs=pl.BlockSpec(memory_space=pltpu.VMEM),
        scratch_shapes=[
            pltpu.VMEM((count, width, krows), jnp.bfloat16),
            pltpu.VMEM(queries.shape, jnp.bfloat16),
            pltpu.VMEM((heads * rows, width), jnp.bfloat16),
            pltpu.VMEM(w_uk.shape, jnp.bfloat16),
            pltpu.VMEM(w_uv.shape, jnp.bfloat16),
            pltpu.VMEM((heads * rows, 128), jnp.float32),
            pltpu.VMEM((heads * rows, 128), jnp.float32),
            pltpu.VMEM((heads * rows, rank), jnp.float32),
            dma((deep, PIECES)),
            dma((deep, lanes, PIECES)),
            dma((deep, PIECES)),
            dma((deep, lanes, PIECES)),
            dma((lanes, PIECES)),
            dma((count, PIECES)),
            dma((3,)),
            dma((4,)),
        ],
        compiler_params=pltpu.CompilerParams(
            collective_id=0, has_side_effects=True, vmem_limit_bytes=55050 * 1024
        ),
    )(queries, latents.T, w_uk, w_uv)


def solution(mesh):
    placed = (P(("groups", "ctx"), None), P(("groups", "ctx"), None), P(), P())
    return jax.shard_map(
        functools.partial(body, mesh.shape["ctx"]),
        mesh=mesh, in_specs=placed, out_specs=P(("groups", "ctx"), None), check_vma=False,
    )
```

```python
import functools
import math

import jax
import jax.numpy as jnp
from jax import lax
from jax.experimental import pallas as pl
from jax.experimental.pallas import tpu as pltpu
from jax.sharding import PartitionSpec as P

CORES = 2
PIECES = 4
HALF = PIECES // 2
MESH = pl.DeviceIdType.MESH


def grid_of(count):
    chips = count // CORES
    wide = 1 << (int(math.log2(chips)) // 3)
    return chips // wide, wide


def kernel(
    deep, wide, heads, nope, rank,
    queries, latents, w_uk, w_uv, out,
    keys, raw, q_all, uk, uv, top, total, acc,
    up_sem, side_sem, twin_sem, pass_sem, far_sem, recv_sem, local_sem, uk_sem,
):
    index = lax.axis_index("ctx")
    core = lax.rem(index, CORES)
    x = lax.rem(index // CORES, wide)
    z = index // (CORES * wide)
    rows = out.shape[0]
    krows = latents.shape[1]
    width = raw.shape[1] // heads
    vdim = out.shape[1] // heads
    span = CORES * krows
    factor = math.log2(math.e) / math.sqrt(width)

    def place(zz, xx, cc):
        return (zz * wide + xx) * CORES + cc

    def piece_of(piece):
        size = keys.shape[1] // PIECES
        return pl.ds(piece * size, size)

    def copy(block, piece, target, send_sem, own=False):
        there = keys.at[block, piece_of(piece), :]
        return pltpu.make_async_remote_copy(
            src_ref=latents.at[piece_of(piece), :] if own else there,
            dst_ref=there,
            send_sem=send_sem,
            recv_sem=recv_sem.at[block, piece],
            device_id={"ctx": target},
            device_id_type=MESH,
        )

    twin = place(z, x, 1 - core)
    above = place(lax.rem(z + 1, deep), x, core)
    below = place(lax.rem(z + deep - 1, deep), x, core)
    sides = [lax.rem(x + d, wide) for d in range(1, wide)]

    groups = uk_sem.shape[0]
    per = heads // groups
    raw_copy = pltpu.make_async_copy(queries, raw, local_sem.at[0])
    raw_copy.start()
    uk_copies = []
    for g in range(groups):
        part = pl.ds(g * per, per)
        uk_copies.append(pltpu.make_async_copy(w_uk.at[part], uk.at[part], uk_sem.at[g]))
        uk_copies[-1].start()
    own_copy = pltpu.make_async_copy(latents, keys.at[index], local_sem.at[1])
    own_copy.start()

    barrier = pltpu.get_barrier_semaphore()

    def greet(target):
        pl.semaphore_signal(barrier, inc=1, device_id={"ctx": target}, device_id_type=MESH)

    greet(twin)
    for side in sides:
        greet(place(z, side, core))

    @pl.when(z + 1 < deep)
    def _():
        greet(above)

    @pl.when(z > 0)
    def _():
        greet(below)

    ends = (z + 1 < deep).astype(jnp.int32) + (z > 0).astype(jnp.int32)
    pl.semaphore_wait(barrier, wide + ends)

    def spread(step, piece, own, act):
        block = place(z - step, x, core)

        @pl.when(z + 1 < deep)
        def _():
            act(copy(block, piece, above, up_sem.at[step, piece], own))

        for d, side in enumerate(sides):
            def to_side():
                act(copy(block, piece, place(z, side, core), side_sem.at[step, d, piece], own))

            if own and piece >= HALF:
                pl.when(jnp.logical_or(side > x, z == 0))(to_side)
            elif own:
                pl.when(side > x)(to_side)
            elif piece >= HALF:
                pl.when(step < z)(to_side)
            else:
                to_side()
        act(copy(block, piece, twin, twin_sem.at[step, piece], own))

    def arrived(block, piece):
        copy(block, piece, twin, twin_sem.at[0, 0]).wait_recv()

    def whole(block):
        for piece in range(PIECES):
            arrived(block, piece)

    def needed(step, side):
        return jnp.logical_or(step >= 1, side < x)

    def column(step, piece):
        arrived(place(z - step, x, core), piece)
        spread(step, piece, False, lambda c: c.start())

    def hand(step, piece, d, side, act):
        act(copy(place(z - step, side, core), piece, twin, pass_sem.at[step, d, piece]))

    def relay(piece, d, side, act):
        @pl.when(z + 1 < deep)
        def _():
            act(copy(place(0, side, core), piece, above, far_sem.at[d, piece]))

    def across(step, piece):
        for d, side in enumerate(sides):
            @pl.when(needed(step, side))
            def _():
                arrived(place(z - step, side, core), piece)
                hand(step, piece, d, side, lambda c: c.start())

    def far(piece):
        for d, side in enumerate(sides):
            arrived(place(0, side, core), piece)
            relay(piece, d, side, lambda c: c.start())

            @pl.when(needed(z, side))
            def _():
                hand(z, piece, d, side, lambda c: c.start())

    for piece in range(PIECES):
        spread(0, piece, True, lambda c: c.start())

    raw_copy.wait()
    uv_copy = pltpu.make_async_copy(w_uv, uv, local_sem.at[2])
    for h in range(heads):
        if h % per == 0:
            uk_copies[h // per].wait()
        query = raw[:, h * width:(h + 1) * width]
        lat = jnp.dot(query[:, :nope], uk[h], preferred_element_type=jnp.float32)
        q_all[h * rows:(h + 1) * rows, :rank] = lat.astype(jnp.bfloat16)
        q_all[h * rows:(h + 1) * rows, rank:] = query[:, nope:]
    uv_copy.start()

    parts = 2
    lanes = top.shape[1]
    high = heads * rows // parts

    def attend(pair, first):
        blocks = [keys[pair * CORES + c] for c in range(CORES)]
        key = jnp.concatenate(blocks, axis=1)
        value = key[:rank, :].T
        owns = [pl.ds(part * high, high) for part in range(parts)]
        scores = [
            jnp.dot(q_all[own, :], key, preferred_element_type=jnp.float32) for own in owns
        ]
        for own, score in zip(owns, scores):
            if first:
                row = lax.broadcasted_iota(jnp.int32, score.shape, 0)
                col = lax.broadcasted_iota(jnp.int32, score.shape, 1)
                limit = core * krows + krows - rows + lax.rem(row, rows)
                score = jnp.where(col <= limit, score, -jnp.inf)
            best = jnp.broadcast_to(jnp.max(score, axis=1, keepdims=True), (high, lanes))
            if not first:
                old = top[own, :]
                best = jnp.maximum(old, best)
            expos = [
                jnp.exp2((score[:, lane:lane + lanes] - best) * factor)
                for lane in range(0, span, lanes)
            ]
            mass = functools.reduce(jnp.add, expos)
            weight = jnp.concatenate([e.astype(jnp.bfloat16) for e in expos], axis=1)
            gain = jnp.dot(weight, value, preferred_element_type=jnp.float32)
            if first:
                total[own, :] = mass
                acc[own, :] = gain
            else:
                shrink = jnp.exp2((old - best) * factor)
                total[own, :] = total[own, :] * shrink + mass
                for lane in range(0, rank, lanes):
                    part = slice(lane, lane + lanes)
                    acc[own, part] = acc[own, part] * shrink + gain[:, part]
            top[own, :] = best

    def attend_column(step):
        whole(place(z - step, x, 1 - core))
        attend((z - step) * wide + x, False)

    def attend_across(step):
        for side in sides:
            @pl.when(needed(step, side))
            def _():
                whole(place(z - step, side, 1 - core))
                attend((z - step) * wide + side, False)

    own_copy.wait()
    whole(twin)
    attend(index // CORES, True)

    low, up = range(HALF), range(HALF, PIECES)

    def step_of(step, carry):
        for piece in low:
            column(step, piece)

        @pl.when(step >= 2)
        def _():
            for piece in up:
                across(step - 2, piece)
            attend_column(step - 1)

        for piece in up:
            column(step, piece)
        for piece in low:
            across(step - 1, piece)

        @pl.when(step >= 2)
        def _():
            attend_across(step - 2)

        return carry

    lax.fori_loop(1, z + 1, step_of, 0)

    @pl.when(z >= 1)
    def _():
        for piece in up:
            across(z - 1, piece)
        attend_column(z)

    for piece in low:
        across(z, piece)
    for piece in up:
        far(piece)

    @pl.when(z >= 1)
    def _():
        attend_across(z - 1)

    attend_across(z)

    uv_copy.wait()
    group = math.gcd(heads, 2)
    for first in range(0, heads, group):
        own = pl.ds(first * rows, group * rows)
        mass = jnp.sum(total[own, :], axis=1, keepdims=True)
        mixed = (acc[own, :] * (1.0 / mass)).astype(jnp.bfloat16)
        wide_uv = jnp.concatenate([uv[first + g] for g in range(group)], axis=1)
        both = jnp.dot(mixed, wide_uv, preferred_element_type=jnp.float32).astype(out.dtype)
        for g in range(group):
            out[:, (first + g) * vdim:(first + g + 1) * vdim] = both[
                g * rows:(g + 1) * rows, g * vdim:(g + 1) * vdim
            ]

    def drain(step, carry):
        for piece in range(PIECES):
            @pl.when(step >= 1)
            def _():
                spread(step, piece, False, lambda c: c.wait_send())

            for d, side in enumerate(sides):
                @pl.when(needed(step, side))
                def _():
                    hand(step, piece, d, side, lambda c: c.wait_send())
        return carry

    for piece in range(PIECES):
        spread(0, piece, True, lambda c: c.wait_send())
    lax.fori_loop(0, z + 1, drain, 0)
    for piece in up:
        for d, side in enumerate(sides):
            relay(piece, d, side, lambda c: c.wait_send())


def body(count, queries, latents, w_uk, w_uv):
    deep, wide = grid_of(count)
    heads, nope, rank = w_uk.shape
    vdim = w_uv.shape[2]
    rows = queries.shape[0]
    krows, width = latents.shape
    dma = pltpu.SemaphoreType.DMA
    lanes = max(wide - 1, 1)
    return pl.pallas_call(
        functools.partial(kernel, deep, wide, heads, nope, rank),
        out_shape=jax.ShapeDtypeStruct((rows, heads * vdim), jnp.bfloat16),
        in_specs=[pl.BlockSpec(memory_space=pltpu.HBM)] * 4,
        out_specs=pl.BlockSpec(memory_space=pltpu.VMEM),
        scratch_shapes=[
            pltpu.VMEM((count, width, krows), jnp.bfloat16),
            pltpu.VMEM(queries.shape, jnp.bfloat16),
            pltpu.VMEM((heads * rows, width), jnp.bfloat16),
            pltpu.VMEM(w_uk.shape, jnp.bfloat16),
            pltpu.VMEM(w_uv.shape, jnp.bfloat16),
            pltpu.VMEM((heads * rows, 128), jnp.float32),
            pltpu.VMEM((heads * rows, 128), jnp.float32),
            pltpu.VMEM((heads * rows, rank), jnp.float32),
            dma((deep, PIECES)),
            dma((deep, lanes, PIECES)),
            dma((deep, PIECES)),
            dma((deep, lanes, PIECES)),
            dma((lanes, PIECES)),
            dma((count, PIECES)),
            dma((3,)),
            dma((4,)),
        ],
        compiler_params=pltpu.CompilerParams(
            collective_id=0, has_side_effects=True, vmem_limit_bytes=55050 * 1024
        ),
    )(queries, latents.T, w_uk, w_uv)


def solution(mesh):
    placed = (P(("groups", "ctx"), None), P(("groups", "ctx"), None), P(), P())
    return jax.shard_map(
        functools.partial(body, mesh.shape["ctx"]),
        mesh=mesh, in_specs=placed, out_specs=P(("groups", "ctx"), None), check_vma=False,
    )
```

```python
import functools
import math

import jax
import jax.numpy as jnp
from jax import lax
from jax.experimental import pallas as pl
from jax.experimental.pallas import tpu as pltpu
from jax.sharding import PartitionSpec as P

CORES = 2
PIECES = 6
HALF = PIECES // 2
MESH = pl.DeviceIdType.MESH


def grid_of(count):
    chips = count // CORES
    wide = 1 << (int(math.log2(chips)) // 3)
    return chips // wide, wide


def kernel(
    deep, wide, heads, nope, rank,
    queries, latents, w_uk, w_uv, out,
    keys, raw, q_all, uk, uv, top, total, acc,
    up_sem, side_sem, twin_sem, pass_sem, far_sem, recv_sem, local_sem, uk_sem,
):
    index = lax.axis_index("ctx")
    core = lax.rem(index, CORES)
    x = lax.rem(index // CORES, wide)
    z = index // (CORES * wide)
    rows = out.shape[0]
    krows = latents.shape[1]
    width = raw.shape[1] // heads
    vdim = out.shape[1] // heads
    span = CORES * krows
    factor = math.log2(math.e) / math.sqrt(width)

    def place(zz, xx, cc):
        return (zz * wide + xx) * CORES + cc

    def piece_of(piece):
        size = keys.shape[1] // PIECES
        return pl.ds(piece * size, size)

    def copy(block, piece, target, send_sem, own=False):
        there = keys.at[block, piece_of(piece), :]
        return pltpu.make_async_remote_copy(
            src_ref=latents.at[piece_of(piece), :] if own else there,
            dst_ref=there,
            send_sem=send_sem,
            recv_sem=recv_sem.at[block, piece],
            device_id={"ctx": target},
            device_id_type=MESH,
        )

    twin = place(z, x, 1 - core)
    above = place(lax.rem(z + 1, deep), x, core)
    below = place(lax.rem(z + deep - 1, deep), x, core)
    sides = [lax.rem(x + d, wide) for d in range(1, wide)]

    groups = uk_sem.shape[0]
    per = heads // groups
    raw_copy = pltpu.make_async_copy(queries, raw, local_sem.at[0])
    raw_copy.start()
    uk_copies = []
    for g in range(groups):
        part = pl.ds(g * per, per)
        uk_copies.append(pltpu.make_async_copy(w_uk.at[part], uk.at[part], uk_sem.at[g]))
        uk_copies[-1].start()
    own_copy = pltpu.make_async_copy(latents, keys.at[index], local_sem.at[1])
    own_copy.start()

    barrier = pltpu.get_barrier_semaphore()

    def greet(target):
        pl.semaphore_signal(barrier, inc=1, device_id={"ctx": target}, device_id_type=MESH)

    greet(twin)
    for side in sides:
        greet(place(z, side, core))

    @pl.when(z + 1 < deep)
    def _():
        greet(above)

    @pl.when(z > 0)
    def _():
        greet(below)

    ends = (z + 1 < deep).astype(jnp.int32) + (z > 0).astype(jnp.int32)
    pl.semaphore_wait(barrier, wide + ends)

    def spread(step, piece, own, act):
        block = place(z - step, x, core)

        @pl.when(z + 1 < deep)
        def _():
            act(copy(block, piece, above, up_sem.at[step, piece], own))

        for d, side in enumerate(sides):
            def to_side():
                act(copy(block, piece, place(z, side, core), side_sem.at[step, d, piece], own))

            if own and piece >= HALF:
                pl.when(jnp.logical_or(side > x, z == 0))(to_side)
            elif own:
                pl.when(side > x)(to_side)
            elif piece >= HALF:
                pl.when(step < z)(to_side)
            else:
                to_side()
        act(copy(block, piece, twin, twin_sem.at[step, piece], own))

    def arrived(block, piece):
        copy(block, piece, twin, twin_sem.at[0, 0]).wait_recv()

    def whole(block):
        for piece in range(PIECES):
            arrived(block, piece)

    def needed(step, side):
        return jnp.logical_or(step >= 1, side < x)

    def column(step, piece):
        arrived(place(z - step, x, core), piece)
        spread(step, piece, False, lambda c: c.start())

    def hand(step, piece, d, side, act):
        act(copy(place(z - step, side, core), piece, twin, pass_sem.at[step, d, piece]))

    def relay(piece, d, side, act):
        @pl.when(z + 1 < deep)
        def _():
            act(copy(place(0, side, core), piece, above, far_sem.at[d, piece]))

    def across(step, piece):
        for d, side in enumerate(sides):
            @pl.when(needed(step, side))
            def _():
                arrived(place(z - step, side, core), piece)
                hand(step, piece, d, side, lambda c: c.start())

    def far(piece):
        for d, side in enumerate(sides):
            arrived(place(0, side, core), piece)
            relay(piece, d, side, lambda c: c.start())

            @pl.when(needed(z, side))
            def _():
                hand(z, piece, d, side, lambda c: c.start())

    for piece in range(PIECES):
        spread(0, piece, True, lambda c: c.start())

    raw_copy.wait()
    uv_copy = pltpu.make_async_copy(w_uv, uv, local_sem.at[2])
    for h in range(heads):
        if h % per == 0:
            uk_copies[h // per].wait()
        query = raw[:, h * width:(h + 1) * width]
        lat = jnp.dot(query[:, :nope], uk[h], preferred_element_type=jnp.float32)
        q_all[h * rows:(h + 1) * rows, :rank] = lat.astype(jnp.bfloat16)
        q_all[h * rows:(h + 1) * rows, rank:] = query[:, nope:]
    uv_copy.start()

    parts = 2
    lanes = top.shape[1]
    high = heads * rows // parts

    def attend(pair, first):
        blocks = [keys[pair * CORES + c] for c in range(CORES)]
        key = jnp.concatenate(blocks, axis=1)
        value = key[:rank, :].T
        owns = [pl.ds(part * high, high) for part in range(parts)]
        scores = [
            jnp.dot(q_all[own, :], key, preferred_element_type=jnp.float32) for own in owns
        ]
        for own, score in zip(owns, scores):
            if first:
                row = lax.broadcasted_iota(jnp.int32, score.shape, 0)
                col = lax.broadcasted_iota(jnp.int32, score.shape, 1)
                limit = core * krows + krows - rows + lax.rem(row, rows)
                score = jnp.where(col <= limit, score, -jnp.inf)
            best = jnp.broadcast_to(jnp.max(score, axis=1, keepdims=True), (high, lanes))
            if not first:
                old = top[own, :]
                best = jnp.maximum(old, best)
            expos = [
                jnp.exp2((score[:, lane:lane + lanes] - best) * factor)
                for lane in range(0, span, lanes)
            ]
            mass = functools.reduce(jnp.add, expos)
            weight = jnp.concatenate([e.astype(jnp.bfloat16) for e in expos], axis=1)
            gain = jnp.dot(weight, value, preferred_element_type=jnp.float32)
            if first:
                total[own, :] = mass
                acc[own, :] = gain
            else:
                shrink = jnp.exp2((old - best) * factor)
                total[own, :] = total[own, :] * shrink + mass
                for lane in range(0, rank, lanes):
                    part = slice(lane, lane + lanes)
                    acc[own, part] = acc[own, part] * shrink + gain[:, part]
            top[own, :] = best

    def attend_column(step):
        whole(place(z - step, x, 1 - core))
        attend((z - step) * wide + x, False)

    def attend_across(step):
        for side in sides:
            @pl.when(needed(step, side))
            def _():
                whole(place(z - step, side, 1 - core))
                attend((z - step) * wide + side, False)

    own_copy.wait()
    whole(twin)
    attend(index // CORES, True)

    low, up = range(HALF), range(HALF, PIECES)

    def step_of(step, carry):
        for piece in low:
            column(step, piece)

        @pl.when(step >= 2)
        def _():
            for piece in up:
                across(step - 2, piece)
            attend_column(step - 1)

        for piece in up:
            column(step, piece)
        for piece in low:
            across(step - 1, piece)

        @pl.when(step >= 2)
        def _():
            attend_across(step - 2)

        return carry

    lax.fori_loop(1, z + 1, step_of, 0)

    @pl.when(z >= 1)
    def _():
        for piece in up:
            across(z - 1, piece)
        attend_column(z)

    for piece in low:
        across(z, piece)
    for piece in up:
        far(piece)

    @pl.when(z >= 1)
    def _():
        attend_across(z - 1)

    attend_across(z)

    uv_copy.wait()
    for h in range(heads):
        own = pl.ds(h * rows, rows)
        mass = jnp.sum(total[own, :], axis=1, keepdims=True)
        mixed = (acc[own, :] * (1.0 / mass)).astype(jnp.bfloat16)
        out[:, h * vdim:(h + 1) * vdim] = jnp.dot(
            mixed, uv[h], preferred_element_type=jnp.float32
        ).astype(out.dtype)

    def drain(step, carry):
        for piece in range(PIECES):
            @pl.when(step >= 1)
            def _():
                spread(step, piece, False, lambda c: c.wait_send())

            for d, side in enumerate(sides):
                @pl.when(needed(step, side))
                def _():
                    hand(step, piece, d, side, lambda c: c.wait_send())
        return carry

    for piece in range(PIECES):
        spread(0, piece, True, lambda c: c.wait_send())
    lax.fori_loop(0, z + 1, drain, 0)
    for piece in up:
        for d, side in enumerate(sides):
            relay(piece, d, side, lambda c: c.wait_send())


def body(count, queries, latents, w_uk, w_uv):
    deep, wide = grid_of(count)
    heads, nope, rank = w_uk.shape
    vdim = w_uv.shape[2]
    rows = queries.shape[0]
    krows, width = latents.shape
    dma = pltpu.SemaphoreType.DMA
    lanes = max(wide - 1, 1)
    return pl.pallas_call(
        functools.partial(kernel, deep, wide, heads, nope, rank),
        out_shape=jax.ShapeDtypeStruct((rows, heads * vdim), jnp.bfloat16),
        in_specs=[pl.BlockSpec(memory_space=pltpu.HBM)] * 4,
        out_specs=pl.BlockSpec(memory_space=pltpu.VMEM),
        scratch_shapes=[
            pltpu.VMEM((count, width, krows), jnp.bfloat16),
            pltpu.VMEM(queries.shape, jnp.bfloat16),
            pltpu.VMEM((heads * rows, width), jnp.bfloat16),
            pltpu.VMEM(w_uk.shape, jnp.bfloat16),
            pltpu.VMEM(w_uv.shape, jnp.bfloat16),
            pltpu.VMEM((heads * rows, 128), jnp.float32),
            pltpu.VMEM((heads * rows, 128), jnp.float32),
            pltpu.VMEM((heads * rows, rank), jnp.float32),
            dma((deep, PIECES)),
            dma((deep, lanes, PIECES)),
            dma((deep, PIECES)),
            dma((deep, lanes, PIECES)),
            dma((lanes, PIECES)),
            dma((count, PIECES)),
            dma((3,)),
            dma((4,)),
        ],
        compiler_params=pltpu.CompilerParams(
            collective_id=0, has_side_effects=True, vmem_limit_bytes=55050 * 1024
        ),
    )(queries, latents.T, w_uk, w_uv)


def solution(mesh):
    placed = (P(("groups", "ctx"), None), P(("groups", "ctx"), None), P(), P())
    return jax.shard_map(
        functools.partial(body, mesh.shape["ctx"]),
        mesh=mesh, in_specs=placed, out_specs=P(("groups", "ctx"), None), check_vma=False,
    )
```
